32 devices in a mesh: freq: 8 (over y, x, core), lat: 4 (over z).
Axes of the slice: x: 2, y: 2, z: 4, core: 2. Of those that a mesh axis runs over, the one named last changes fastest.
Arguments:
- record: float32 [8, 2, 4, 4096], P(None, None, 'lat', 'freq'), may hold values from -6 to 6
- receiver_cell: int32 [4, 4096], P('lat'), may hold values from 0 to 131071
- source_cell: int32 [1], replicated, may hold values from 0 to 524287
- wavelet: float32 [8, 2], P('freq'), may hold values from -4 to 4
- frequency_index: int32 [8], P('freq'), may hold values from 8 to 199
- slowness: float32 [2, 512, 1024], P(None, 'lat', 'freq'), may hold values from 0.000222 to 0.000667
- anisotropy: float32 [2, 512, 1024], P(None, 'lat', 'freq'), may hold values from 0.05 to 0.4
- reference_slowness: float32 [2], replicated, may hold values from 0.00025 to 0.00059
- reference_anisotropy: float32 [2], replicated, may hold values from 0.05 to 0.3
- correction_block: bfloat16 [2, 128, 128], replicated, may hold values from -0.31 to 1.61
Outputs:
- migrated_image: float32 [2, 512, 1024], P(None, 'lat', 'freq')
- wavefields: bfloat16 [2, 8, 2, 512, 1024], P(None, 'freq', None, 'lat')
The draws below stay inside these ranges and needn't reach their ends.
All inputs are finite; a program needn't handle non-finite values.
Results may differ from the reference program's by a relative error of at most 0.034.
Values may be sent and summed in bfloat16 or wider, within the bound.
A program may use at most 256 MiB of HBM per device.

```python
import math
import jax
import jax.numpy as jnp
from jax import lax

NX = 1024
NY = 512
STEPS = 2
BLOCK = 128
NF = 8
TR_GRP = 4096
SLAB = 128
N_LAT = 4


def draw_correction_block(key, part):
    diag_key, off_key = jax.random.split(jax.random.fold_in(key, 11))
    diagonal = jax.random.uniform(diag_key, (STEPS, BLOCK), jnp.float32, 0.6, 1.4)
    spread = jnp.clip(0.05 * jax.random.normal(off_key, (STEPS, BLOCK, BLOCK), jnp.float32), -0.3, 0.3)
    identity = jnp.eye(BLOCK, dtype=jnp.float32)
    matrix = spread * (1.0 - identity) + diagonal[:, :, None] * identity
    return matrix.astype(jnp.bfloat16)


def plant(entries, stream_key, smallest, high):
    longest = entries.shape.index(max(entries.shape))
    spots = []
    for shift in (0, 1):
        where = [jax.random.randint(jax.random.fold_in(stream_key, axis), (), 0, length) for axis, length in enumerate(entries.shape)]
        where[longest] = (where[longest] + shift) % entries.shape[longest]
        spots.append(tuple(where))
    return entries.at[spots[0]].set(smallest).at[spots[1]].set(high)


def shard_levels(own_key, extent, shards, low, top_value):
    def one(dim, parts):
        heights = jax.random.uniform(jax.random.fold_in(jax.random.fold_in(own_key, 6), dim), (parts,), jnp.float32, low / len(shards), top_value / len(shards))
        return jnp.repeat(jnp.exp(heights), extent[dim] // parts).reshape((-1,) + (1,) * (len(extent) - dim - 1))

    loudness = one(*shards[0])
    for cut in shards[1:]:
        loudness = loudness * one(*cut)
    return loudness


def noise(key, dims, scale, reach, shards=(), kind=jnp.bfloat16):
    entries = scale * jax.random.normal(key, dims, jnp.float32)
    if shards:
        entries = entries * shard_levels(key, dims, shards, -0.22, 0.18)
    return jnp.clip(entries, -reach, reach).astype(kind)


def setup_inputs(seed: int = 0) -> dict:
    splits = jax.random.split(jax.random.key(seed), 11)
    record = noise(splits[0], (NF, 2, N_LAT, TR_GRP), 1.0, 6.0, ((2, 4), (3, 8)), jnp.float32)
    receiver_cell = plant(jax.random.randint(splits[1], (N_LAT, TR_GRP), 0, SLAB * NX), jax.random.fold_in(splits[1], 1), 0, (SLAB * NX) - 1).astype(jnp.int32)
    source_cell = jax.random.randint(splits[2], (1,), 0, NY * NX).astype(jnp.int32)
    wavelet = noise(splits[3], (NF, 2), 1.0, 4.0, ((0, 8),), jnp.float32)
    frequency_index = plant(jax.random.randint(splits[4], (NF,), 8, 200), jax.random.fold_in(splits[4], 1), 8, 199).astype(jnp.int32)
    slowness = jnp.clip(jnp.exp(math.log(0.000667) - 1.1001127 * jax.random.uniform(splits[5], (STEPS, NY, NX), jnp.float32) ** shard_levels(splits[5], (STEPS, NY, NX), ((1, 4), (2, 8)), -0.2, 0.2)), 0.000222, 0.000667)
    anisotropy = jnp.clip(0.05 + 0.35 * jax.random.uniform(splits[6], (STEPS, NY, NX), jnp.float32) ** shard_levels(splits[6], (STEPS, NY, NX), ((1, 4), (2, 8)), -0.2, 0.2), 0.05, 0.4)
    reference_slowness = jnp.clip(jnp.exp(jax.random.uniform(splits[7], (STEPS,), jnp.float32, math.log(0.00025), math.log(0.00059))), 0.00025, 0.00059)
    reference_anisotropy = jnp.clip(jax.random.uniform(splits[8], (STEPS,), jnp.float32, 0.05, 0.3), 0.05, 0.3)
    correction_block = draw_correction_block(jax.random.fold_in(splits[10], 71), 0)
    return {"record": record, "receiver_cell": receiver_cell, "source_cell": source_cell, "wavelet": wavelet, "frequency_index": frequency_index, "slowness": slowness, "anisotropy": anisotropy, "reference_slowness": reference_slowness, "reference_anisotropy": reference_anisotropy, "correction_block": correction_block}


grid_step = 10.0
depth_step = 10.0
freq_step = 0.25
datum_depth = 2000.0
water_slowness = 1.0 / 1500.0

def transform_table(length, direction):
    indices = jnp.arange(length, dtype=jnp.int32)
    products = indices[:, None] * indices[None, :] % length
    angles = products.astype(jnp.float32) * (2.0 * math.pi / length)
    factor = 1.0 / math.sqrt(length)
    cosine = jnp.cos(angles) * factor
    sine_part = direction * jnp.sin(angles) * factor
    top_rows = jnp.stack([cosine, sine_part], axis=1)
    low_rows = jnp.stack([-sine_part, cosine], axis=1)
    return jnp.stack([top_rows, low_rows], axis=0).astype(jnp.bfloat16)

def wavenumber(indices, length):
    signed = jnp.where(indices < length // 2, indices, indices - length)
    return signed.astype(jnp.float32) * (2.0 * math.pi / (length * grid_step))

def source_field(wavelet, angular, line_index, cell_index, source_cell, width):
    source_line = source_cell[0] // width
    source_col = source_cell[0] - source_line * width
    off_line = (line_index - source_line).astype(jnp.float32) * grid_step
    off_col = (cell_index - source_col).astype(jnp.float32) * grid_step
    radius = jnp.sqrt(off_line[:, None] ** 2 + off_col[None, :] ** 2 + datum_depth ** 2)
    amplitude = datum_depth / radius
    phase = angular[:, None, None] * (radius * water_slowness)[None]
    cosine = amplitude[None] * jnp.cos(phase)
    sine_part = amplitude[None] * jnp.sin(phase)
    wave_real = wavelet[:, 0][:, None, None]
    wave_imag = wavelet[:, 1][:, None, None]
    real_part = wave_real * cosine - wave_imag * sine_part
    imag_part = wave_real * sine_part + wave_imag * cosine
    return jnp.stack([real_part, imag_part], axis=1)

def rotate(wavefield, cosine, sine_part):
    field_sign = jnp.array([1.0, -1.0], jnp.float32).reshape(2, 1, 1, 1)
    signed_sine = sine_part[None] * field_sign
    real_part = wavefield[:, :, 0]
    imag_part = wavefield[:, :, 1]
    next_real = real_part * cosine[None] - imag_part * signed_sine
    next_imag = imag_part * cosine[None] + real_part * signed_sine
    return jnp.stack([next_real, next_imag], axis=2)

def propagate(spectrum, angular, wave_y, wave_x, slow_ref, aniso_ref):
    lateral = wave_y[:, None] ** 2 + wave_x[None, :] ** 2
    vertical = ((angular * slow_ref) ** 2)[:, None, None] - (1.0 + 2.0 * aniso_ref) * lateral[None]
    real_root = jnp.sqrt(jnp.maximum(vertical, 0.0))
    decay_root = jnp.sqrt(jnp.maximum(-vertical, 0.0))
    damping = jnp.exp(-decay_root * depth_step)
    return rotate(spectrum, damping * jnp.cos(real_root * depth_step), damping * jnp.sin(real_root * depth_step))

def correct(space, angular, slow_now, aniso_now, slow_ref, block):
    phases = angular[:, None, None] * (slow_now - slow_ref)[None] * depth_step
    split = rotate(space, jnp.cos(phases), jnp.sin(phases)).astype(jnp.bfloat16)
    shape = split.shape
    width = block.shape[0]
    blocks = split.astype(jnp.float32).reshape(shape[:4] + (shape[4] // width, width))
    correction = jnp.einsum('gfcajb,bd->gfcajd', blocks, block.astype(jnp.float32)).reshape(shape)
    coefficient = angular[:, None, None] * (slow_now * aniso_now)[None] * depth_step
    field_sign = jnp.array([1.0, -1.0], jnp.float32).reshape(2, 1, 1, 1)
    scaled = coefficient[None] * field_sign
    base = split.astype(jnp.float32)
    next_real = base[:, :, 0] - scaled * correction[:, :, 1]
    next_imag = base[:, :, 1] + scaled * correction[:, :, 0]
    return jnp.stack([next_real, next_imag], axis=2).astype(jnp.bfloat16)

def reference(record, receiver_cell, source_cell, wavelet, frequency_index, slowness, anisotropy, reference_slowness, reference_anisotropy, correction_block):
    slab_cells = NY // N_LAT * NX
    offsets = (jnp.arange(N_LAT, dtype=jnp.int32) * slab_cells)[:, None]
    targets = (receiver_cell + offsets).reshape(-1)
    values = record.reshape(NF * 2, -1)
    receiver = jnp.zeros((NF * 2, NY * NX), jnp.float32).at[:, targets].add(values)
    receiver = receiver.reshape(NF, 2, NY, NX)
    angular = frequency_index.astype(jnp.float32) * (2.0 * math.pi * freq_step)
    source = source_field(wavelet, angular, jnp.arange(NY, dtype=jnp.int32), jnp.arange(NX, dtype=jnp.int32), source_cell, NX)
    wavefield = jnp.stack([source, receiver]).astype(jnp.bfloat16)
    forward_x = transform_table(NX, -1.0).astype(jnp.float32)
    inverse_x = transform_table(NX, 1.0).astype(jnp.float32)
    forward_y = transform_table(NY, -1.0).astype(jnp.float32)
    inverse_y = transform_table(NY, 1.0).astype(jnp.float32)
    wave_x = wavenumber(jnp.arange(NX, dtype=jnp.int32), NX)
    wave_y = wavenumber(jnp.arange(NY, dtype=jnp.int32), NY)
    images = []
    for depth_index in range(STEPS):
        x_spectrum = jnp.einsum('gfcyx,cxdk->gfdyk', wavefield.astype(jnp.float32), forward_x).astype(jnp.bfloat16)
        spectrum = jnp.einsum('gfcyx,cydk->gfdkx', x_spectrum.astype(jnp.float32), forward_y)
        shifted = propagate(spectrum, angular, wave_y, wave_x, reference_slowness[depth_index], reference_anisotropy[depth_index]).astype(jnp.bfloat16)
        back_rows = jnp.einsum('gfcyx,cydk->gfdkx', shifted.astype(jnp.float32), inverse_y).astype(jnp.bfloat16)
        space = jnp.einsum('gfcyx,cxdk->gfdyk', back_rows.astype(jnp.float32), inverse_x)
        wavefield = correct(space, angular, slowness[depth_index], anisotropy[depth_index], reference_slowness[depth_index], correction_block[depth_index])
        wide = wavefield.astype(jnp.float32)
        images.append(lax.optimization_barrier(jnp.sum(wide[0, :, 0] * wide[1, :, 0] + wide[0, :, 1] * wide[1, :, 1], axis=0)))
    return (jnp.stack(images), wavefield)
```

```python
import functools
import math

import jax
import jax.numpy as jnp
import ml_dtypes
import numpy as np
from jax import lax
from jax.experimental import pallas as pl
from jax.experimental.pallas import tpu as pltpu
from jax.sharding import PartitionSpec as P

NX = 1024
NY = 512
STEPS = 2
SLAB = 128
TILE = 256
HALF = 512

grid_step = 10.0
depth_step = 10.0
freq_step = 0.25
datum_depth = 2000.0
water_slowness = 1.0 / 1500.0
f32 = jnp.float32
bf16 = jnp.bfloat16
VMEM_LIMIT = 50 * 1024 * 1024


def trig(length):
    idx = np.arange(length)
    ang = (idx[:, None] * idx[None, :] % length) * (2.0 * math.pi / length)
    return np.cos(ang) / math.sqrt(length), np.sin(ang) / math.sqrt(length)


def tables():
    cx, sx = trig(NX)
    xt = np.stack([cx, sx]).astype(ml_dtypes.bfloat16)
    cy, sy = trig(NY)
    rows = np.arange(NY).reshape(2, 2, SLAB)
    fwd = []
    for s in range(2):
        ys = rows[:, s].reshape(-1)
        c, e = cy[:, ys], -sy[:, ys]
        fwd.append(np.block([[c, -e], [e, c]]))
    inv = []
    for hi in range(2):
        per = []
        for s in range(2):
            c, e = cy[rows[hi, s]], sy[rows[hi, s]]
            per.append(np.block([[c, -e], [e, c]]))
        inv.append(np.stack(per))
    return (
        xt,
        np.stack(fwd).astype(ml_dtypes.bfloat16),
        np.stack(inv).astype(ml_dtypes.bfloat16),
    )


def cos_poly(z, terms):
    acc = jnp.full_like(z, (-1.0) ** terms / math.factorial(2 * terms))
    for k in range(terms - 1, -1, -1):
        acc = acc * z + (-1.0) ** k / math.factorial(2 * k)
    return acc


def sinc_poly(z, terms):
    acc = jnp.full_like(z, (-1.0) ** terms / math.factorial(2 * terms + 1))
    for k in range(terms - 1, -1, -1):
        acc = acc * z + (-1.0) ** k / math.factorial(2 * k + 1)
    return acc


def call(kernel, grid, in_specs, out_specs, out_shape, scratch=(), flops=0):
    return pl.pallas_call(
        kernel,
        out_shape=out_shape,
        grid_spec=pltpu.PrefetchScalarGridSpec(
            num_scalar_prefetch=2,
            grid=grid,
            in_specs=in_specs,
            out_specs=out_specs,
            scratch_shapes=list(scratch),
        ),
        compiler_params=pltpu.CompilerParams(vmem_limit_bytes=VMEM_LIMIT),
        cost_estimate=pl.CostEstimate(
            flops=flops, bytes_accessed=4 * 1024 * 1024, transcendentals=0
        ),
    )


def start_kernel(ints, reals, cell_ref, value_ref, out_ref, acc):
    core = ints[0]
    slab = 2 * pl.program_id(0) + core
    traces = cell_ref.shape[-1]
    chunk = 512
    acc[...] = jnp.zeros_like(acc)

    def add(i, carry):
        at = pl.ds(pl.multiple_of(i * chunk, chunk), chunk)
        cells = cell_ref[0, :, at]
        line = cells // NX
        col = cells - line * NX
        ylines = lax.broadcasted_iota(jnp.int32, (SLAB, chunk), 0)
        hit = ylines == line
        vals = value_ref[0, :, at].astype(f32)
        left = jnp.concatenate(
            [jnp.where(hit, vals[c : c + 1], 0.0).astype(bf16) for c in range(2)], axis=0
        )
        for j in range(NX // TILE):
            xcols = lax.broadcasted_iota(jnp.int32, (TILE, chunk), 0) + j * TILE
            right = jnp.where(xcols == col, 1.0, 0.0).astype(bf16)
            acc[:, j * TILE : (j + 1) * TILE] += lax.dot_general(
                left, right, (((1,), (1,)), ((), ())), preferred_element_type=f32
            )
        return carry

    lax.fori_loop(0, traces // chunk, add, 0)
    out_ref[1] = acc[...].astype(bf16).reshape(2, SLAB, NX)

    strip = 32

    def source(i, carry):
        at = pl.ds(pl.multiple_of(i * strip, strip), strip)
        line = lax.broadcasted_iota(jnp.int32, (strip, NX), 0) + (
            slab * SLAB + i * strip - ints[2]
        )
        col = lax.broadcasted_iota(jnp.int32, (strip, NX), 1) - ints[3]
        dy = line.astype(f32) * grid_step
        dx = col.astype(f32) * grid_step
        radius = jnp.sqrt(dy * dy + dx * dx + datum_depth**2)
        amplitude = datum_depth / radius
        phase = reals[0] * (radius * water_slowness)
        turns = jnp.floor(phase * (0.5 / math.pi) + 0.5)
        rest = phase - turns * 6.28125
        rest = rest - turns * (2.0 * math.pi - 6.28125)
        z = rest * rest
        cosine = amplitude * cos_poly(z, 9)
        sine = amplitude * (rest * sinc_poly(z, 9))
        out_ref[0, 0, at, :] = (reals[1] * cosine - reals[2] * sine).astype(bf16)
        out_ref[0, 1, at, :] = (reals[1] * sine + reals[2] * cosine).astype(bf16)
        return carry

    lax.fori_loop(0, SLAB // strip, source, 0)


def start_fields(ints, reals, cells, values):
    traces = cells.shape[-1]
    return call(
        start_kernel,
        (2,),
        [
            pl.BlockSpec((1, 1, traces), lambda i, a, b: (2 * i + a[0], 0, 0)),
            pl.BlockSpec((1, 2, traces), lambda i, a, b: (2 * i + a[0], 0, 0)),
        ],
        pl.BlockSpec((2, 2, SLAB, NX), lambda i, a, b: (0, 0, i, 0)),
        jax.ShapeDtypeStruct((2, 2, 2 * SLAB, NX), bf16),
        [pltpu.VMEM((2 * SLAB, NX), f32)],
        flops=8_000_000_000,
    )(ints, reals, cells, values)


def forward_x_kernel(ints, reals, wave_ref, table_ref, out_ref):
    rows = wave_ref.shape[2]
    left = wave_ref[...].reshape(4 * rows, NX)
    cos_part = jnp.dot(left, table_ref[0], preferred_element_type=f32)
    sin_part = jnp.dot(left, table_ref[1], preferred_element_type=f32)
    cos_part = cos_part.reshape(2, 2, rows, -1)
    sin_part = sin_part.reshape(2, 2, rows, -1)
    out_ref[:, 0] = (cos_part[:, 0] + sin_part[:, 1]).astype(bf16)
    out_ref[:, 1] = (cos_part[:, 1] - sin_part[:, 0]).astype(bf16)


def forward_x(ints, reals, wave, table, other):
    def half(a):
        return (1 - a[0]) if other else a[0]

    rows = wave.shape[2]
    tiles = HALF // TILE
    return call(
        forward_x_kernel,
        (tiles,),
        [
            pl.BlockSpec((2, 2, rows, NX), lambda i, a, b: (0, 0, 0, 0)),
            pl.BlockSpec((2, NX, TILE), lambda i, a, b: (0, 0, half(a) * tiles + i)),
        ],
        pl.BlockSpec((2, 2, rows, TILE), lambda i, a, b: (0, 0, 0, i)),
        jax.ShapeDtypeStruct((2, 2, rows, HALF), bf16),
        flops=4_000_000_000,
    )(ints, reals, wave, table)


def middle_kernel(
    step, ints, reals, mine_ref, got_ref, fm_ref, fg_ref, im_ref, ig_ref, keep_ref, send_ref
):
    width = mine_ref.shape[-1]
    omega, slow, aniso = reals[0], reals[3 + step], reals[3 + STEPS + step]
    q = lax.broadcasted_iota(jnp.int32, (NY, width), 0)
    k = lax.broadcasted_iota(jnp.int32, (NY, width), 1)
    k = k + ints[0] * HALF + pl.program_id(0) * width
    q = jnp.where(q < NY // 2, q, q - NY).astype(f32) * (2.0 * math.pi / (NY * grid_step))
    k = jnp.where(k < NX // 2, k, k - NX).astype(f32) * (2.0 * math.pi / (NX * grid_step))
    base = omega * slow
    vertical = base * base - (1.0 + 2.0 * aniso) * (q * q + k * k)
    going = jnp.maximum(vertical, 0.0)
    z = going * (depth_step * depth_step)
    damping = jnp.exp(jnp.sqrt(jnp.maximum(-vertical, 0.0)) * (-depth_step))
    cosine = damping * cos_poly(z, 8)
    sine = damping * (jnp.sqrt(going) * depth_step * sinc_poly(z, 8))
    slabs = im_ref.shape[0]
    for g in range(2):
        spec = jnp.dot(
            fm_ref[0], mine_ref[g].reshape(4 * SLAB, width), preferred_element_type=f32
        ) + jnp.dot(fg_ref[0], got_ref[g].reshape(4 * SLAB, width), preferred_element_type=f32)
        re, im = spec[:NY], spec[NY:]
        sgn = sine if g == 0 else -sine
        shifted = jnp.concatenate(
            [(re * cosine - im * sgn).astype(bf16), (im * cosine + re * sgn).astype(bf16)], axis=0
        )
        for hi in range(slabs):
            at = slice(hi * SLAB, (hi + 1) * SLAB)
            for table, out in ((ig_ref, send_ref), (im_ref, keep_ref)):
                back = jnp.dot(table[hi, 0], shifted, preferred_element_type=f32).astype(bf16)
                out[g, 0, at] = back[:SLAB]
                out[g, 1, at] = back[SLAB:]


def middle(step, ints, reals, mine, got, fwd, inv):
    last = step == STEPS - 1
    slabs = 1 if last else 2
    rows = slabs * SLAB

    def low(a):
        return a[1] if last else 0

    width = TILE
    return call(
        functools.partial(middle_kernel, step),
        (HALF // width,),
        [
            pl.BlockSpec((2, 2, 2 * SLAB, width), lambda i, a, b: (0, 0, 0, i)),
            pl.BlockSpec((2, 2, 2 * SLAB, width), lambda i, a, b: (0, 0, 0, i)),
            pl.BlockSpec((1, 2 * NY, NY), lambda i, a, b: (a[0], 0, 0)),
            pl.BlockSpec((1, 2 * NY, NY), lambda i, a, b: (1 - a[0], 0, 0)),
            pl.BlockSpec((slabs, 1, 2 * SLAB, 2 * NY), lambda i, a, b: (low(a), a[0], 0, 0)),
            pl.BlockSpec((slabs, 1, 2 * SLAB, 2 * NY), lambda i, a, b: (low(a), 1 - a[0], 0, 0)),
        ],
        [pl.BlockSpec((2, 2, rows, width), lambda i, a, b: (0, 0, 0, i))] * 2,
        [jax.ShapeDtypeStruct((2, 2, rows, HALF), bf16)] * 2,
        flops=4_000_000_000,
    )(ints, reals, mine, got, fwd, fwd, inv, inv)


def inverse_x_kernel(
    step, ints, reals, keep_ref, got_ref, tm_ref, tg_ref, model_ref, block_ref, wave_ref, image_ref
):
    rows = keep_ref.shape[2]
    mine = keep_ref[...].reshape(4 * rows, HALF)
    got = got_ref[...].reshape(4 * rows, HALF)
    omega, slow_ref = reals[0], reals[3 + step]
    cos_part = jnp.dot(mine, tm_ref[0], preferred_element_type=f32) + jnp.dot(
        got, tg_ref[0], preferred_element_type=f32
    )
    sin_part = jnp.dot(mine, tm_ref[1], preferred_element_type=f32) + jnp.dot(
        got, tg_ref[1], preferred_element_type=f32
    )
    cos_part = cos_part.reshape(2, 2, rows, TILE)
    sin_part = sin_part.reshape(2, 2, rows, TILE)
    space_re = cos_part[:, 0] - sin_part[:, 1]
    space_im = cos_part[:, 1] + sin_part[:, 0]
    matrix = block_ref[step]
    width = matrix.shape[0]
    slabs = rows // SLAB
    for j in range(TILE // width):
        at = slice(j * width, (j + 1) * width)
        model = model_ref[j].astype(f32)
        slow = model[:, 0, 0].reshape(rows, width)
        aniso = model[:, 0, 1].reshape(rows, width)
        phase = omega * (slow - slow_ref) * depth_step
        z = phase * phase
        cosine = cos_poly(z, 7)
        sine = phase * sinc_poly(z, 7)
        coefficient = omega * (slow * aniso) * depth_step
        nexts = []
        for g in range(2):
            sgn = sine if g == 0 else -sine
            re, im = space_re[g, :, at], space_im[g, :, at]
            split_re = (re * cosine - im * sgn).astype(bf16)
            split_im = (im * cosine + re * sgn).astype(bf16)
            both = jnp.concatenate([split_re, split_im], axis=0)
            correction = jnp.dot(both, matrix, preferred_element_type=f32)
            scaled = coefficient if g == 0 else -coefficient
            next_re = (split_re.astype(f32) - scaled * correction[rows:]).astype(bf16)
            next_im = (split_im.astype(f32) + scaled * correction[:rows]).astype(bf16)
            wave_ref[g, 0, :, at] = next_re
            wave_ref[g, 1, :, at] = next_im
            nexts.append((next_re.astype(f32), next_im.astype(f32)))
        image = nexts[0][0] * nexts[1][0] + nexts[0][1] * nexts[1][1]
        image_ref[:, at] = image.astype(bf16)


def inverse_x(step, ints, reals, keep, got, table, model, block):
    last = step == STEPS - 1
    rows = keep.shape[2]
    slabs = rows // SLAB
    width = block.shape[-1]

    def low(a):
        return a[1] if last else 0

    return call(
        functools.partial(inverse_x_kernel, step),
        (NX // TILE,),
        [
            pl.BlockSpec((2, 2, rows, HALF), lambda i, a, b: (0, 0, 0, 0)),
            pl.BlockSpec((2, 2, rows, HALF), lambda i, a, b: (0, 0, 0, 0)),
            pl.BlockSpec((2, HALF, TILE), lambda i, a, b: (0, a[0], i)),
            pl.BlockSpec((2, HALF, TILE), lambda i, a, b: (0, 1 - a[0], i)),
            pl.BlockSpec(
                (TILE // width, slabs, 1, 2, SLAB, width),
                lambda i, a, b: (i, low(a), a[0], 0, 0, 0),
            ),
            pl.BlockSpec((STEPS, width, width), lambda i, a, b: (0, 0, 0)),
        ],
        [
            pl.BlockSpec((2, 2, rows, TILE), lambda i, a, b: (0, 0, 0, i)),
            pl.BlockSpec((rows, TILE), lambda i, a, b: (0, i)),
        ],
        [
            jax.ShapeDtypeStruct((2, 2, rows, NX), bf16),
            jax.ShapeDtypeStruct((rows, NX), bf16),
        ],
        flops=5_000_000_000,
    )(ints, reals, keep, got, table, table, model, block)


def body(
    nfreq,
    nlat,
    record,
    receiver_cell,
    source_cell,
    wavelet,
    frequency_index,
    slowness,
    anisotropy,
    reference_slowness,
    reference_anisotropy,
    correction_block,
):
    fi = lax.axis_index("freq")
    zi = lax.axis_index("lat")
    core = fi % 2
    zh = zi // 2
    fc = zi % 2
    own = fi - core + fc
    pair = [(i, i ^ 1) for i in range(nfreq)]
    swap = [
        ((2 * j + h) * nlat + 2 * a + c, (2 * j + c) * nlat + 2 * a + h)
        for j in range(nfreq // 2)
        for h in range(2)
        for a in range(nlat // 2)
        for c in range(2)
    ]
    xt, fwd, inv = (jnp.asarray(t) for t in tables())

    head = jnp.concatenate(
        [frequency_index.astype(f32), wavelet.reshape(-1)]
    )
    head_other = lax.ppermute(head, "freq", pair)
    head = jnp.where(core == fc, head, head_other)
    angular = head[0] * (2.0 * math.pi * freq_step)

    both = ("freq", "lat")
    values = lax.all_gather(record.astype(bf16), both)
    cells = lax.all_gather(receiver_cell, "lat")
    nrec = values.shape[-1]
    values = values.reshape((nfreq, nlat) + values.shape[1:3] + (nrec,))
    values = lax.dynamic_index_in_dim(values, own, 2, keepdims=False)
    values = values.transpose(1, 2, 0, 3).reshape(nlat, 2, nfreq * nrec)

    models = []
    for s in range(STEPS):
        model = jnp.stack([slowness[s], anisotropy[s]]).astype(bf16)
        model = lax.all_gather(model, both)
        width = model.shape[-1]
        model = model.reshape(nfreq, 2, 2, 2, SLAB, width)
        if width != SLAB:
            model = model.transpose(1, 2, 3, 4, 0, 5).reshape(2, 2, 2, SLAB, NX // SLAB, SLAB)
            model = model.transpose(4, 0, 1, 2, 3, 5)
        models.append(model)

    source_line = source_cell[0] // NX
    ints = jnp.stack([core, zh, source_line, source_cell[0] - source_line * NX]).astype(jnp.int32)
    reals = jnp.concatenate(
        [angular[None], head[1:3], reference_slowness, reference_anisotropy]
    )
    wave = start_fields(ints, reals, cells, values)
    images = []
    for s in range(STEPS):
        send = forward_x(ints, reals, wave, xt, True)
        got = lax.ppermute(send, "freq", pair)
        mine = forward_x(ints, reals, wave, xt, False)
        keep, send = middle(s, ints, reals, mine, got, fwd, inv)
        got = lax.ppermute(send, "freq", pair)
        wave, image = inverse_x(s, ints, reals, keep, got, xt, models[s], correction_block)
        if s < STEPS - 1:
            image = lax.dynamic_slice_in_dim(image, zh * SLAB, SLAB, 0)
        image = lax.ppermute(image, both, swap)
        image = lax.all_to_all(image, "freq", split_axis=1, concat_axis=0, tiled=True)
        image = image.reshape(nfreq, SLAB, NX // nfreq).astype(f32)
        images.append(jnp.sum(image, axis=0))
    wave = lax.ppermute(wave, both, swap)
    return jnp.stack(images), wave[:, None]


def solution(mesh):
    return jax.shard_map(
        functools.partial(body, mesh.shape["freq"], mesh.shape["lat"]),
        mesh=mesh,
        in_specs=(
            P(None, None, "lat", "freq"),
            P("lat", None),
            P(),
            P("freq", None),
            P("freq"),
            P(None, "lat", "freq"),
            P(None, "lat", "freq"),
            P(),
            P(),
            P(),
        ),
        out_specs=(P(None, "lat", "freq"), P(None, "freq", None, "lat", None)),
        check_vma=False,
    )
```

```python
import functools
import math

import jax
import jax.numpy as jnp
import ml_dtypes
import numpy as np
from jax import lax
from jax.experimental import pallas as pl
from jax.experimental.pallas import tpu as pltpu
from jax.sharding import PartitionSpec as P

NX = 1024
NY = 512
STEPS = 2
SLAB = 128
TILE = 256
HALF = 512

grid_step = 10.0
depth_step = 10.0
freq_step = 0.25
datum_depth = 2000.0
water_slowness = 1.0 / 1500.0
f32 = jnp.float32
bf16 = jnp.bfloat16
VMEM_LIMIT = 28 * 1024 * 1024


def trig(length):
    idx = np.arange(length)
    ang = (idx[:, None] * idx[None, :] % length) * (2.0 * math.pi / length)
    return np.cos(ang) / math.sqrt(length), np.sin(ang) / math.sqrt(length)


def tables():
    cx, sx = trig(NX)
    xt = np.stack([cx, sx]).astype(ml_dtypes.bfloat16)
    cy, sy = trig(NY)
    rows = np.arange(NY).reshape(2, 2, SLAB)
    fwd = []
    for s in range(2):
        ys = rows[:, s].reshape(-1)
        c, e = cy[:, ys], -sy[:, ys]
        fwd.append(np.block([[c, -e], [e, c]]))
    inv = []
    for hi in range(2):
        per = []
        for s in range(2):
            c, e = cy[rows[hi, s]], sy[rows[hi, s]]
            per.append(np.block([[c, -e], [e, c]]))
        inv.append(np.stack(per))
    return (
        xt,
        np.stack(fwd).astype(ml_dtypes.bfloat16),
        np.stack(inv).astype(ml_dtypes.bfloat16),
    )


def cos_poly(z, terms):
    acc = jnp.full_like(z, (-1.0) ** terms / math.factorial(2 * terms))
    for k in range(terms - 1, -1, -1):
        acc = acc * z + (-1.0) ** k / math.factorial(2 * k)
    return acc


def sinc_poly(z, terms):
    acc = jnp.full_like(z, (-1.0) ** terms / math.factorial(2 * terms + 1))
    for k in range(terms - 1, -1, -1):
        acc = acc * z + (-1.0) ** k / math.factorial(2 * k + 1)
    return acc


def call(kernel, grid, in_specs, out_specs, out_shape, scratch=(), flops=0):
    return pl.pallas_call(
        kernel,
        out_shape=out_shape,
        grid_spec=pltpu.PrefetchScalarGridSpec(
            num_scalar_prefetch=2,
            grid=grid,
            in_specs=in_specs,
            out_specs=out_specs,
            scratch_shapes=list(scratch),
        ),
        compiler_params=pltpu.CompilerParams(vmem_limit_bytes=VMEM_LIMIT),
        cost_estimate=pl.CostEstimate(
            flops=flops, bytes_accessed=4 * 1024 * 1024, transcendentals=0
        ),
    )


def start_kernel(ints, reals, packet_ref, out_ref, acc):
    core = ints[0]
    slab = 2 * pl.program_id(0) + core
    traces = packet_ref.shape[-1]
    chunk = 512
    acc[...] = jnp.zeros_like(acc)

    def add(i, carry):
        at = pl.ds(pl.multiple_of(i * chunk, chunk), chunk)
        cells = packet_ref[0, 2:3, at].astype(jnp.int32)
        line = cells // NX
        col = cells - line * NX
        ylines = lax.broadcasted_iota(jnp.int32, (SLAB, chunk), 0)
        hit = ylines == line
        vals = packet_ref[0, 0:2, at]
        left = jnp.concatenate(
            [jnp.where(hit, vals[c : c + 1], 0.0).astype(bf16) for c in range(2)], axis=0
        )
        for j in range(NX // TILE):
            xcols = lax.broadcasted_iota(jnp.int32, (TILE, chunk), 0) + j * TILE
            right = jnp.where(xcols == col, 1.0, 0.0).astype(bf16)
            acc[:, j * TILE : (j + 1) * TILE] += lax.dot_general(
                left, right, (((1,), (1,)), ((), ())), preferred_element_type=f32
            )
        return carry

    lax.fori_loop(0, traces // chunk, add, 0)
    out_ref[1] = acc[...].astype(bf16).reshape(2, SLAB, NX)

    strip = 32

    def source(i, carry):
        at = pl.ds(pl.multiple_of(i * strip, strip), strip)
        line = lax.broadcasted_iota(jnp.int32, (strip, NX), 0) + (
            slab * SLAB + i * strip - ints[2]
        )
        col = lax.broadcasted_iota(jnp.int32, (strip, NX), 1) - ints[3]
        dy = line.astype(f32) * grid_step
        dx = col.astype(f32) * grid_step
        radius = jnp.sqrt(dy * dy + dx * dx + datum_depth**2)
        amplitude = datum_depth / radius
        phase = reals[0] * (radius * water_slowness)
        turns = jnp.floor(phase * (0.5 / math.pi) + 0.5)
        rest = phase - turns * 6.28125
        rest = rest - turns * (2.0 * math.pi - 6.28125)
        z = rest * rest
        cosine = amplitude * cos_poly(z, 9)
        sine = amplitude * (rest * sinc_poly(z, 9))
        out_ref[0, 0, at, :] = (reals[1] * cosine - reals[2] * sine).astype(bf16)
        out_ref[0, 1, at, :] = (reals[1] * sine + reals[2] * cosine).astype(bf16)
        return carry

    lax.fori_loop(0, SLAB // strip, source, 0)


def start_fields(ints, reals, packets):
    traces = packets.shape[-1]
    return call(
        start_kernel,
        (2,),
        [pl.BlockSpec((1, 4, traces), lambda i, a, b: (i + a[1] - 2 * i * a[1], 0, 0))],
        pl.BlockSpec((2, 2, SLAB, NX), lambda i, a, b: (0, 0, i, 0)),
        jax.ShapeDtypeStruct((2, 2, 2 * SLAB, NX), bf16),
        [pltpu.VMEM((2 * SLAB, NX), f32)],
        flops=8_000_000_000,
    )(ints, reals, packets)


def forward_x_kernel(ints, reals, wave_ref, table_ref, out_ref):
    rows = wave_ref.shape[2]
    left = wave_ref[...].reshape(4 * rows, NX)
    cos_part = jnp.dot(left, table_ref[0], preferred_element_type=f32)
    sin_part = jnp.dot(left, table_ref[1], preferred_element_type=f32)
    cos_part = cos_part.reshape(2, 2, rows, -1)
    sin_part = sin_part.reshape(2, 2, rows, -1)
    out_ref[:, 0] = (cos_part[:, 0] + sin_part[:, 1]).astype(bf16)
    out_ref[:, 1] = (cos_part[:, 1] - sin_part[:, 0]).astype(bf16)


def forward_x(ints, reals, wave, table, other):
    def half(a):
        return (1 - a[0]) if other else a[0]

    rows = wave.shape[2]
    tiles = HALF // TILE
    return call(
        forward_x_kernel,
        (tiles,),
        [
            pl.BlockSpec((2, 2, rows, NX), lambda i, a, b: (0, 0, 0, 0)),
            pl.BlockSpec((2, NX, TILE), lambda i, a, b: (0, 0, half(a) * tiles + i)),
        ],
        pl.BlockSpec((2, 2, rows, TILE), lambda i, a, b: (0, 0, 0, i)),
        jax.ShapeDtypeStruct((2, 2, rows, HALF), bf16),
        flops=4_000_000_000,
    )(ints, reals, wave, table)


def middle_kernel(
    step, ints, reals, mine_ref, got_ref, fm_ref, fg_ref, im_ref, ig_ref, keep_ref, send_ref
):
    width = mine_ref.shape[-1]
    omega, slow, aniso = reals[0], reals[3 + step], reals[3 + STEPS + step]
    q = lax.broadcasted_iota(jnp.int32, (NY, width), 0)
    k = lax.broadcasted_iota(jnp.int32, (NY, width), 1)
    k = k + ints[0] * HALF + pl.program_id(0) * width
    q = jnp.where(q < NY // 2, q, q - NY).astype(f32) * (2.0 * math.pi / (NY * grid_step))
    k = jnp.where(k < NX // 2, k, k - NX).astype(f32) * (2.0 * math.pi / (NX * grid_step))
    base = omega * slow
    vertical = base * base - (1.0 + 2.0 * aniso) * (q * q + k * k)
    going = jnp.maximum(vertical, 0.0)
    z = going * (depth_step * depth_step)
    damping = jnp.exp(jnp.sqrt(jnp.maximum(-vertical, 0.0)) * (-depth_step))
    cosine = damping * cos_poly(z, 8)
    sine = damping * (jnp.sqrt(going) * depth_step * sinc_poly(z, 8))
    slabs = im_ref.shape[0]
    for g in range(2):
        spec = jnp.dot(
            fm_ref[0], mine_ref[g].reshape(4 * SLAB, width), preferred_element_type=f32
        ) + jnp.dot(fg_ref[0], got_ref[g].reshape(4 * SLAB, width), preferred_element_type=f32)
        re, im = spec[:NY], spec[NY:]
        sgn = sine if g == 0 else -sine
        shifted = jnp.concatenate(
            [(re * cosine - im * sgn).astype(bf16), (im * cosine + re * sgn).astype(bf16)], axis=0
        )
        for hi in range(slabs):
            at = slice(hi * SLAB, (hi + 1) * SLAB)
            for table, out in ((ig_ref, send_ref), (im_ref, keep_ref)):
                back = jnp.dot(table[hi, 0], shifted, preferred_element_type=f32).astype(bf16)
                out[g, 0, at] = back[:SLAB]
                out[g, 1, at] = back[SLAB:]


def middle(step, ints, reals, mine, got, fwd, inv):
    last = step == STEPS - 1
    slabs = 1 if last else 2
    rows = slabs * SLAB

    def low(a):
        return a[1] if last else 0

    width = TILE
    return call(
        functools.partial(middle_kernel, step),
        (HALF // width,),
        [
            pl.BlockSpec((2, 2, 2 * SLAB, width), lambda i, a, b: (0, 0, 0, i)),
            pl.BlockSpec((2, 2, 2 * SLAB, width), lambda i, a, b: (0, 0, 0, i)),
            pl.BlockSpec((1, 2 * NY, NY), lambda i, a, b: (a[0], 0, 0)),
            pl.BlockSpec((1, 2 * NY, NY), lambda i, a, b: (1 - a[0], 0, 0)),
            pl.BlockSpec((slabs, 1, 2 * SLAB, 2 * NY), lambda i, a, b: (low(a), a[0], 0, 0)),
            pl.BlockSpec((slabs, 1, 2 * SLAB, 2 * NY), lambda i, a, b: (low(a), 1 - a[0], 0, 0)),
        ],
        [pl.BlockSpec((2, 2, rows, width), lambda i, a, b: (0, 0, 0, i))] * 2,
        [jax.ShapeDtypeStruct((2, 2, rows, HALF), bf16)] * 2,
        flops=4_000_000_000,
    )(ints, reals, mine, got, fwd, fwd, inv, inv)


def inverse_x_kernel(
    step, ints, reals, keep_ref, got_ref, tm_ref, tg_ref, *refs
):
    *model_refs, block_ref, wave_ref, image_ref = refs
    rows = keep_ref.shape[2]
    mine = keep_ref[...].reshape(4 * rows, HALF)
    got = got_ref[...].reshape(4 * rows, HALF)
    omega, slow_ref = reals[0], reals[3 + step]
    cos_part = jnp.dot(mine, tm_ref[0], preferred_element_type=f32) + jnp.dot(
        got, tg_ref[0], preferred_element_type=f32
    )
    sin_part = jnp.dot(mine, tm_ref[1], preferred_element_type=f32) + jnp.dot(
        got, tg_ref[1], preferred_element_type=f32
    )
    cos_part = cos_part.reshape(2, 2, rows, TILE)
    sin_part = sin_part.reshape(2, 2, rows, TILE)
    space_re = cos_part[:, 0] - sin_part[:, 1]
    space_im = cos_part[:, 1] + sin_part[:, 0]
    matrix = block_ref[step]
    width = matrix.shape[0]
    slabs = rows // SLAB
    for j in range(TILE // width):
        at = slice(j * width, (j + 1) * width)
        near = model_refs[0][j].astype(f32)
        if slabs == 1:
            slow, aniso = near[0], near[1]
        else:
            far = model_refs[1][j].astype(f32)
            first = jnp.where(ints[1] == 0, near, far)
            second = jnp.where(ints[1] == 0, far, near)
            slow = jnp.concatenate([first[0], second[0]], axis=0)
            aniso = jnp.concatenate([first[1], second[1]], axis=0)
        phase = omega * (slow - slow_ref) * depth_step
        z = phase * phase
        cosine = cos_poly(z, 7)
        sine = phase * sinc_poly(z, 7)
        coefficient = omega * (slow * aniso) * depth_step
        nexts = []
        for g in range(2):
            sgn = sine if g == 0 else -sine
            re, im = space_re[g, :, at], space_im[g, :, at]
            split_re = (re * cosine - im * sgn).astype(bf16)
            split_im = (im * cosine + re * sgn).astype(bf16)
            both = jnp.concatenate([split_re, split_im], axis=0)
            correction = jnp.dot(both, matrix, preferred_element_type=f32)
            scaled = coefficient if g == 0 else -coefficient
            next_re = (split_re.astype(f32) - scaled * correction[rows:]).astype(bf16)
            next_im = (split_im.astype(f32) + scaled * correction[:rows]).astype(bf16)
            wave_ref[g, 0, :, at] = next_re
            wave_ref[g, 1, :, at] = next_im
            nexts.append((next_re.astype(f32), next_im.astype(f32)))
        image = nexts[0][0] * nexts[1][0] + nexts[0][1] * nexts[1][1]
        image_ref[:, at] = image.astype(bf16)


def inverse_x(step, ints, reals, keep, got, table, model, block):
    rows = keep.shape[2]
    width = block.shape[-1]

    return call(
        functools.partial(inverse_x_kernel, step),
        (NX // TILE,),
        [
            pl.BlockSpec((2, 2, rows, HALF), lambda i, a, b: (0, 0, 0, 0)),
            pl.BlockSpec((2, 2, rows, HALF), lambda i, a, b: (0, 0, 0, 0)),
            pl.BlockSpec((2, HALF, TILE), lambda i, a, b: (0, a[0], i)),
            pl.BlockSpec((2, HALF, TILE), lambda i, a, b: (0, 1 - a[0], i)),
        ]
        + [pl.BlockSpec((TILE // width, 2, SLAB, width), lambda i, a, b: (i, 0, 0, 0))]
        * len(model)
        + [
            pl.BlockSpec((STEPS, width, width), lambda i, a, b: (0, 0, 0)),
        ],
        [
            pl.BlockSpec((2, 2, rows, TILE), lambda i, a, b: (0, 0, 0, i)),
            pl.BlockSpec((rows, TILE), lambda i, a, b: (0, i)),
        ],
        [
            jax.ShapeDtypeStruct((2, 2, rows, NX), bf16),
            jax.ShapeDtypeStruct((rows, NX), bf16),
        ],
        flops=5_000_000_000,
    )(ints, reals, keep, got, table, table, *model, block)


def body(
    nfreq,
    nlat,
    record,
    receiver_cell,
    source_cell,
    wavelet,
    frequency_index,
    slowness,
    anisotropy,
    reference_slowness,
    reference_anisotropy,
    correction_block,
):
    fi = lax.axis_index("freq")
    zi = lax.axis_index("lat")
    core = fi % 2
    zh = zi // 2
    pair = [(i, i ^ 1) for i in range(nfreq)]
    swap = [
        ((2 * j + h) * nlat + 2 * a + c, (2 * j + c) * nlat + 2 * a + h)
        for j in range(nfreq // 2)
        for h in range(2)
        for a in range(nlat // 2)
        for c in range(2)
    ]
    cross = [
        ((2 * j + h) * nlat + 2 * a + c, (2 * j + c) * nlat + 2 * (1 - a) + h)
        for j in range(nfreq // 2)
        for h in range(2)
        for a in range(nlat // 2)
        for c in range(2)
    ]
    xt, fwd, inv = (jnp.asarray(t) for t in tables())

    both = ("freq", "lat")
    moved = lax.all_to_all(record.astype(bf16), "freq", split_axis=0, concat_axis=3, tiled=True)
    traces = receiver_cell.shape[-1]
    scalars = jnp.concatenate([frequency_index.astype(f32), wavelet.reshape(-1)])
    packet = jnp.concatenate(
        [
            moved.reshape(2, traces).astype(f32),
            receiver_cell.astype(f32),
            jnp.pad(scalars, (0, traces - 3))[None],
        ]
    )
    near = lax.ppermute(packet, both, swap)
    far = lax.ppermute(packet, both, cross)
    packets = jnp.stack([near, far])
    head = near[3, :3]
    angular = head[0] * (2.0 * math.pi * freq_step)

    models = []
    for s in range(STEPS):
        model = jnp.stack([slowness[s], anisotropy[s]]).astype(bf16)
        model = lax.all_gather(model, "freq")
        width = model.shape[-1]
        if width != SLAB:
            model = model.transpose(1, 2, 0, 3).reshape(2, SLAB, NX // SLAB, SLAB)
            model = model.transpose(2, 0, 1, 3)
        model_near = lax.ppermute(model, both, swap)
        model = [model_near] if s == STEPS - 1 else [model_near, lax.ppermute(model, both, cross)]
        models.append(model)

    source_line = source_cell[0] // NX
    ints = jnp.stack([core, zh, source_line, source_cell[0] - source_line * NX]).astype(jnp.int32)
    reals = jnp.concatenate(
        [angular[None], head[1:3], reference_slowness, reference_anisotropy]
    )
    wave = start_fields(ints, reals, packets)
    images = []
    for s in range(STEPS):
        send = forward_x(ints, reals, wave, xt, True)
        got = lax.ppermute(send, "freq", pair)
        mine = forward_x(ints, reals, wave, xt, False)
        keep, send = middle(s, ints, reals, mine, got, fwd, inv)
        got = lax.ppermute(send, "freq", pair)
        wave, image = inverse_x(s, ints, reals, keep, got, xt, models[s], correction_block)
        if s < STEPS - 1:
            image = lax.dynamic_slice_in_dim(image, zh * SLAB, SLAB, 0)
        images.append(image)
    images = lax.ppermute(jnp.stack(images), both, swap)
    images = lax.all_to_all(
        images.reshape(STEPS, SLAB, nfreq, NX // nfreq).transpose(2, 0, 1, 3), "freq", 0, 0, tiled=True
    )
    wave = lax.ppermute(wave, both, swap)
    return jnp.sum(images.astype(f32), axis=0), wave[:, None]


def solution(mesh):
    return jax.shard_map(
        functools.partial(body, mesh.shape["freq"], mesh.shape["lat"]),
        mesh=mesh,
        in_specs=(
            P(None, None, "lat", "freq"),
            P("lat", None),
            P(),
            P("freq", None),
            P("freq"),
            P(None, "lat", "freq"),
            P(None, "lat", "freq"),
            P(),
            P(),
            P(),
        ),
        out_specs=(P(None, "lat", "freq"), P(None, "freq", None, "lat", None)),
        check_vma=False,
    )
```

```python
import functools
import math

import jax
import jax.numpy as jnp
import ml_dtypes
import numpy as np
from jax import lax
from jax.experimental import pallas as pl
from jax.experimental.pallas import tpu as pltpu
from jax.sharding import PartitionSpec as P

NX = 1024
NY = 512
STEPS = 2
SLAB = 128
TILE = 256
HALF = 512

grid_step = 10.0
depth_step = 10.0
freq_step = 0.25
datum_depth = 2000.0
water_slowness = 1.0 / 1500.0
f32 = jnp.float32
bf16 = jnp.bfloat16
VMEM_LIMIT = 28 * 1024 * 1024


def trig(length):
    idx = np.arange(length)
    ang = (idx[:, None] * idx[None, :] % length) * (2.0 * math.pi / length)
    return np.cos(ang) / math.sqrt(length), np.sin(ang) / math.sqrt(length)


def tables():
    cx, sx = trig(NX)
    xt = np.stack([cx, sx]).astype(ml_dtypes.bfloat16)
    cy, sy = trig(NY)
    rows = np.arange(NY).reshape(2, 2, SLAB)
    fwd = []
    for s in range(2):
        ys = rows[:, s].reshape(-1)
        c, e = cy[:, ys], -sy[:, ys]
        fwd.append(np.block([[c, -e], [e, c]]))
    inv = []
    for hi in range(2):
        per = []
        for s in range(2):
            c, e = cy[rows[hi, s]], sy[rows[hi, s]]
            per.append(np.block([[c, -e], [e, c]]))
        inv.append(np.stack(per))
    return (
        xt,
        np.stack(fwd).astype(ml_dtypes.bfloat16),
        np.stack(inv).astype(ml_dtypes.bfloat16),
    )


def cos_poly(z, terms):
    acc = jnp.full_like(z, (-1.0) ** terms / math.factorial(2 * terms))
    for k in range(terms - 1, -1, -1):
        acc = acc * z + (-1.0) ** k / math.factorial(2 * k)
    return acc


def sinc_poly(z, terms):
    acc = jnp.full_like(z, (-1.0) ** terms / math.factorial(2 * terms + 1))
    for k in range(terms - 1, -1, -1):
        acc = acc * z + (-1.0) ** k / math.factorial(2 * k + 1)
    return acc


def call(kernel, grid, in_specs, out_specs, out_shape, scratch=(), flops=0):
    return pl.pallas_call(
        kernel,
        out_shape=out_shape,
        grid_spec=pltpu.PrefetchScalarGridSpec(
            num_scalar_prefetch=2,
            grid=grid,
            in_specs=in_specs,
            out_specs=out_specs,
            scratch_shapes=list(scratch),
        ),
        compiler_params=pltpu.CompilerParams(vmem_limit_bytes=VMEM_LIMIT),
        cost_estimate=pl.CostEstimate(
            flops=flops, bytes_accessed=4 * 1024 * 1024, transcendentals=0
        ),
    )


def start_kernel(ints, reals, packet_ref, out_ref, acc):
    core = ints[0]
    slab = 2 * pl.program_id(0) + core
    traces = packet_ref.shape[-1]
    chunk = 512
    acc[...] = jnp.zeros_like(acc)

    def add(i, carry):
        at = pl.ds(pl.multiple_of(i * chunk, chunk), chunk)
        cells = packet_ref[0, 2:3, at].astype(jnp.int32)
        line = cells // NX
        col = cells - line * NX
        ylines = lax.broadcasted_iota(jnp.int32, (SLAB, chunk), 0)
        hit = ylines == line
        vals = packet_ref[0, 0:2, at]
        left = jnp.concatenate(
            [jnp.where(hit, vals[c : c + 1], 0.0).astype(bf16) for c in range(2)], axis=0
        )
        for j in range(NX // TILE):
            xcols = lax.broadcasted_iota(jnp.int32, (TILE, chunk), 0) + j * TILE
            right = jnp.where(xcols == col, 1.0, 0.0).astype(bf16)
            acc[:, j * TILE : (j + 1) * TILE] += lax.dot_general(
                left, right, (((1,), (1,)), ((), ())), preferred_element_type=f32
            )
        return carry

    lax.fori_loop(0, traces // chunk, add, 0)
    out_ref[1] = acc[...].astype(bf16).reshape(2, SLAB, NX)

    strip = 32

    def source(i, carry):
        at = pl.ds(pl.multiple_of(i * strip, strip), strip)
        line = lax.broadcasted_iota(jnp.int32, (strip, NX), 0) + (
            slab * SLAB + i * strip - ints[2]
        )
        col = lax.broadcasted_iota(jnp.int32, (strip, NX), 1) - ints[3]
        dy = line.astype(f32) * grid_step
        dx = col.astype(f32) * grid_step
        radius = jnp.sqrt(dy * dy + dx * dx + datum_depth**2)
        amplitude = datum_depth / radius
        phase = reals[0] * (radius * water_slowness)
        turns = jnp.floor(phase * (0.5 / math.pi) + 0.5)
        rest = phase - turns * 6.28125
        rest = rest - turns * (2.0 * math.pi - 6.28125)
        z = rest * rest
        cosine = amplitude * cos_poly(z, 9)
        sine = amplitude * (rest * sinc_poly(z, 9))
        out_ref[0, 0, at, :] = (reals[1] * cosine - reals[2] * sine).astype(bf16)
        out_ref[0, 1, at, :] = (reals[1] * sine + reals[2] * cosine).astype(bf16)
        return carry

    lax.fori_loop(0, SLAB // strip, source, 0)


def start_fields(ints, reals, packets):
    traces = packets.shape[-1]
    return call(
        start_kernel,
        (2,),
        [pl.BlockSpec((1, 4, traces), lambda i, a, b: (i + a[1] - 2 * i * a[1], 0, 0))],
        pl.BlockSpec((2, 2, SLAB, NX), lambda i, a, b: (0, 0, i, 0)),
        jax.ShapeDtypeStruct((2, 2, 2 * SLAB, NX), bf16),
        [pltpu.VMEM((2 * SLAB, NX), f32)],
        flops=8_000_000_000,
    )(ints, reals, packets)


def forward_x_kernel(ints, reals, wave_ref, table_ref, out_ref):
    rows = wave_ref.shape[2]
    left = wave_ref[...].reshape(4 * rows, NX)
    cos_part = jnp.dot(left, table_ref[0], preferred_element_type=f32)
    sin_part = jnp.dot(left, table_ref[1], preferred_element_type=f32)
    cos_part = cos_part.reshape(2, 2, rows, -1)
    sin_part = sin_part.reshape(2, 2, rows, -1)
    out_ref[:, 0] = (cos_part[:, 0] + sin_part[:, 1]).astype(bf16)
    out_ref[:, 1] = (cos_part[:, 1] - sin_part[:, 0]).astype(bf16)


def forward_x(ints, reals, wave, table, other):
    def half(a):
        return (1 - a[0]) if other else a[0]

    rows = wave.shape[2]
    tiles = HALF // TILE
    return call(
        forward_x_kernel,
        (tiles,),
        [
            pl.BlockSpec((2, 2, rows, NX), lambda i, a, b: (0, 0, 0, 0)),
            pl.BlockSpec((2, NX, TILE), lambda i, a, b: (0, 0, half(a) * tiles + i)),
        ],
        pl.BlockSpec((2, 2, rows, TILE), lambda i, a, b: (0, 0, 0, i)),
        jax.ShapeDtypeStruct((2, 2, rows, HALF), bf16),
        flops=4_000_000_000,
    )(ints, reals, wave, table)


def middle_kernel(
    step, ints, reals, mine_ref, got_ref, fm_ref, fg_ref, im_ref, ig_ref, keep_ref, send_ref
):
    width = mine_ref.shape[-1]
    omega, slow, aniso = reals[0], reals[3 + step], reals[3 + STEPS + step]
    q = lax.broadcasted_iota(jnp.int32, (NY, width), 0)
    k = lax.broadcasted_iota(jnp.int32, (NY, width), 1)
    k = k + ints[0] * HALF + pl.program_id(0) * width
    q = jnp.where(q < NY // 2, q, q - NY).astype(f32) * (2.0 * math.pi / (NY * grid_step))
    k = jnp.where(k < NX // 2, k, k - NX).astype(f32) * (2.0 * math.pi / (NX * grid_step))
    base = omega * slow
    vertical = base * base - (1.0 + 2.0 * aniso) * (q * q + k * k)
    going = jnp.maximum(vertical, 0.0)
    z = going * (depth_step * depth_step)
    damping = jnp.exp(jnp.sqrt(jnp.maximum(-vertical, 0.0)) * (-depth_step))
    cosine = damping * cos_poly(z, 8)
    sine = damping * (jnp.sqrt(going) * depth_step * sinc_poly(z, 8))
    slabs = im_ref.shape[0]
    for g in range(2):
        spec = jnp.dot(
            fm_ref[0], mine_ref[g].reshape(4 * SLAB, width), preferred_element_type=f32
        ) + jnp.dot(fg_ref[0], got_ref[g].reshape(4 * SLAB, width), preferred_element_type=f32)
        re, im = spec[:NY], spec[NY:]
        sgn = sine if g == 0 else -sine
        shifted = jnp.concatenate(
            [(re * cosine - im * sgn).astype(bf16), (im * cosine + re * sgn).astype(bf16)], axis=0
        )
        for hi in range(slabs):
            at = slice(hi * SLAB, (hi + 1) * SLAB)
            for table, out in ((ig_ref, send_ref), (im_ref, keep_ref)):
                back = jnp.dot(table[hi, 0], shifted, preferred_element_type=f32).astype(bf16)
                out[g, 0, at] = back[:SLAB]
                out[g, 1, at] = back[SLAB:]


def middle(step, ints, reals, mine, got, fwd, inv):
    last = step == STEPS - 1
    slabs = 1 if last else 2
    rows = slabs * SLAB

    def low(a):
        return a[1] if last else 0

    width = TILE
    return call(
        functools.partial(middle_kernel, step),
        (HALF // width,),
        [
            pl.BlockSpec((2, 2, 2 * SLAB, width), lambda i, a, b: (0, 0, 0, i)),
            pl.BlockSpec((2, 2, 2 * SLAB, width), lambda i, a, b: (0, 0, 0, i)),
            pl.BlockSpec((1, 2 * NY, NY), lambda i, a, b: (a[0], 0, 0)),
            pl.BlockSpec((1, 2 * NY, NY), lambda i, a, b: (1 - a[0], 0, 0)),
            pl.BlockSpec((slabs, 1, 2 * SLAB, 2 * NY), lambda i, a, b: (low(a), a[0], 0, 0)),
            pl.BlockSpec((slabs, 1, 2 * SLAB, 2 * NY), lambda i, a, b: (low(a), 1 - a[0], 0, 0)),
        ],
        [pl.BlockSpec((2, 2, rows, width), lambda i, a, b: (0, 0, 0, i))] * 2,
        [jax.ShapeDtypeStruct((2, 2, rows, HALF), bf16)] * 2,
        flops=4_000_000_000,
    )(ints, reals, mine, got, fwd, fwd, inv, inv)


def inverse_x_kernel(
    step, ints, reals, keep_ref, got_ref, tm_ref, tg_ref, *refs
):
    *model_refs, block_ref, wave_ref, image_ref = refs
    rows = keep_ref.shape[2]
    mine = keep_ref[...].reshape(4 * rows, HALF)
    got = got_ref[...].reshape(4 * rows, HALF)
    omega, slow_ref = reals[0], reals[3 + step]
    cos_part = jnp.dot(mine, tm_ref[0], preferred_element_type=f32) + jnp.dot(
        got, tg_ref[0], preferred_element_type=f32
    )
    sin_part = jnp.dot(mine, tm_ref[1], preferred_element_type=f32) + jnp.dot(
        got, tg_ref[1], preferred_element_type=f32
    )
    cos_part = cos_part.reshape(2, 2, rows, TILE)
    sin_part = sin_part.reshape(2, 2, rows, TILE)
    space_re = cos_part[:, 0] - sin_part[:, 1]
    space_im = cos_part[:, 1] + sin_part[:, 0]
    matrix = block_ref[step]
    width = matrix.shape[0]
    slabs = rows // SLAB
    for j in range(TILE // width):
        at = slice(j * width, (j + 1) * width)
        near = model_refs[0][j].astype(f32)
        if slabs == 1:
            slow, aniso = near[0], near[1]
        else:
            far = model_refs[1][j].astype(f32)
            first = jnp.where(ints[1] == 0, near, far)
            second = jnp.where(ints[1] == 0, far, near)
            slow = jnp.concatenate([first[0], second[0]], axis=0)
            aniso = jnp.concatenate([first[1], second[1]], axis=0)
        phase = omega * (slow - slow_ref) * depth_step
        z = phase * phase
        cosine = cos_poly(z, 7)
        sine = phase * sinc_poly(z, 7)
        coefficient = omega * (slow * aniso) * depth_step
        nexts = []
        for g in range(2):
            sgn = sine if g == 0 else -sine
            re, im = space_re[g, :, at], space_im[g, :, at]
            split_re = (re * cosine - im * sgn).astype(bf16)
            split_im = (im * cosine + re * sgn).astype(bf16)
            both = jnp.concatenate([split_re, split_im], axis=0)
            correction = jnp.dot(both, matrix, preferred_element_type=f32)
            scaled = coefficient if g == 0 else -coefficient
            next_re = (split_re.astype(f32) - scaled * correction[rows:]).astype(bf16)
            next_im = (split_im.astype(f32) + scaled * correction[:rows]).astype(bf16)
            wave_ref[g, 0, :, at] = next_re
            wave_ref[g, 1, :, at] = next_im
            nexts.append((next_re.astype(f32), next_im.astype(f32)))
        image = nexts[0][0] * nexts[1][0] + nexts[0][1] * nexts[1][1]
        image_ref[:, at] = image.astype(bf16)


def inverse_x(step, ints, reals, keep, got, table, model, block):
    rows = keep.shape[2]
    width = block.shape[-1]

    return call(
        functools.partial(inverse_x_kernel, step),
        (NX // TILE,),
        [
            pl.BlockSpec((2, 2, rows, HALF), lambda i, a, b: (0, 0, 0, 0)),
            pl.BlockSpec((2, 2, rows, HALF), lambda i, a, b: (0, 0, 0, 0)),
            pl.BlockSpec((2, HALF, TILE), lambda i, a, b: (0, a[0], i)),
            pl.BlockSpec((2, HALF, TILE), lambda i, a, b: (0, 1 - a[0], i)),
        ]
        + [pl.BlockSpec((TILE // width, 2, SLAB, width), lambda i, a, b: (i, 0, 0, 0))]
        * len(model)
        + [
            pl.BlockSpec((STEPS, width, width), lambda i, a, b: (0, 0, 0)),
        ],
        [
            pl.BlockSpec((2, 2, rows, TILE), lambda i, a, b: (0, 0, 0, i)),
            pl.BlockSpec((rows, TILE), lambda i, a, b: (0, i)),
        ],
        [
            jax.ShapeDtypeStruct((2, 2, rows, NX), bf16),
            jax.ShapeDtypeStruct((rows, NX), bf16),
        ],
        flops=5_000_000_000,
    )(ints, reals, keep, got, table, table, *model, block)


def body(
    nfreq,
    nlat,
    record,
    receiver_cell,
    source_cell,
    wavelet,
    frequency_index,
    slowness,
    anisotropy,
    reference_slowness,
    reference_anisotropy,
    correction_block,
):
    fi = lax.axis_index("freq")
    zi = lax.axis_index("lat")
    core = fi % 2
    zh = zi // 2
    pair = [(i, i ^ 1) for i in range(nfreq)]
    swap = [
        ((2 * j + h) * nlat + 2 * a + c, (2 * j + c) * nlat + 2 * a + h)
        for j in range(nfreq // 2)
        for h in range(2)
        for a in range(nlat // 2)
        for c in range(2)
    ]
    cross = [
        ((2 * j + h) * nlat + 2 * a + c, (2 * j + c) * nlat + 2 * (1 - a) + h)
        for j in range(nfreq // 2)
        for h in range(2)
        for a in range(nlat // 2)
        for c in range(2)
    ]
    xt, fwd, inv = (jnp.asarray(t) for t in tables())

    both = ("freq", "lat")
    gathered = jnp.stack([m[s] for s in range(STEPS) for m in (slowness, anisotropy)])
    gathered = lax.all_gather(gathered.astype(bf16), "freq")
    gathered, record = lax.optimization_barrier((gathered, record))

    moved = lax.all_to_all(record.astype(bf16), "freq", split_axis=0, concat_axis=3, tiled=True)
    traces = receiver_cell.shape[-1]
    scalars = jnp.concatenate([frequency_index.astype(f32), wavelet.reshape(-1)])
    packet = jnp.concatenate(
        [
            moved.reshape(2, traces).astype(f32),
            receiver_cell.astype(f32),
            jnp.pad(scalars, (0, traces - 3))[None],
        ]
    )
    near = lax.ppermute(packet, both, swap)
    far = lax.ppermute(packet, both, cross)
    packets = jnp.stack([near, far])
    head = near[3, :3]
    angular = head[0] * (2.0 * math.pi * freq_step)

    models = []
    for s in range(STEPS):
        model = gathered[:, 2 * s : 2 * s + 2]
        width = model.shape[-1]
        if width != SLAB:
            model = model.transpose(1, 2, 0, 3).reshape(2, SLAB, NX // SLAB, SLAB)
            model = model.transpose(2, 0, 1, 3)
        model_near = lax.ppermute(model, both, swap)
        model = [model_near] if s == STEPS - 1 else [model_near, lax.ppermute(model, both, cross)]
        models.append(model)

    source_line = source_cell[0] // NX
    ints = jnp.stack([core, zh, source_line, source_cell[0] - source_line * NX]).astype(jnp.int32)
    reals = jnp.concatenate(
        [angular[None], head[1:3], reference_slowness, reference_anisotropy]
    )
    wave = start_fields(ints, reals, packets)
    images = []
    for s in range(STEPS):
        send = forward_x(ints, reals, wave, xt, True)
        got = lax.ppermute(send, "freq", pair)
        mine = forward_x(ints, reals, wave, xt, False)
        keep, send = middle(s, ints, reals, mine, got, fwd, inv)
        got = lax.ppermute(send, "freq", pair)
        wave, image = inverse_x(s, ints, reals, keep, got, xt, models[s], correction_block)
        if s < STEPS - 1:
            image = lax.dynamic_slice_in_dim(image, zh * SLAB, SLAB, 0)
        images.append(image)
    images = lax.ppermute(jnp.stack(images), both, swap)
    images = lax.all_to_all(
        images.reshape(STEPS, SLAB, nfreq, NX // nfreq).transpose(2, 0, 1, 3), "freq", 0, 0, tiled=True
    )
    wave = lax.ppermute(wave, both, swap)
    return jnp.sum(images.astype(f32), axis=0), wave[:, None]


def solution(mesh):
    return jax.shard_map(
        functools.partial(body, mesh.shape["freq"], mesh.shape["lat"]),
        mesh=mesh,
        in_specs=(
            P(None, None, "lat", "freq"),
            P("lat", None),
            P(),
            P("freq", None),
            P("freq"),
            P(None, "lat", "freq"),
            P(None, "lat", "freq"),
            P(),
            P(),
            P(),
        ),
        out_specs=(P(None, "lat", "freq"), P(None, "freq", None, "lat", None)),
        check_vma=False,
    )
```

```python
import functools
import math

import jax
import jax.numpy as jnp
import ml_dtypes
import numpy as np
from jax import lax
from jax.experimental import pallas as pl
from jax.experimental.pallas import tpu as pltpu
from jax.sharding import PartitionSpec as P

NX = 1024
NY = 512
STEPS = 2
SLAB = 128
TILE = 256
HALF = 512

grid_step = 10.0
depth_step = 10.0
freq_step = 0.25
datum_depth = 2000.0
water_slowness = 1.0 / 1500.0
f32 = jnp.float32
bf16 = jnp.bfloat16
VMEM_LIMIT = 28 * 1024 * 1024


def trig(length):
    idx = np.arange(length)
    ang = (idx[:, None] * idx[None, :] % length) * (2.0 * math.pi / length)
    return np.cos(ang) / math.sqrt(length), np.sin(ang) / math.sqrt(length)


def tables():
    cx, sx = trig(NX)
    xt = np.stack([cx, sx]).astype(ml_dtypes.bfloat16)
    cy, sy = trig(NY)
    rows = np.arange(NY).reshape(2, 2, SLAB)
    fwd = []
    for s in range(2):
        ys = rows[:, s].reshape(-1)
        c, e = cy[:, ys], -sy[:, ys]
        fwd.append(np.block([[c, -e], [e, c]]))
    inv = []
    for hi in range(2):
        per = []
        for s in range(2):
            c, e = cy[rows[hi, s]], sy[rows[hi, s]]
            per.append(np.block([[c, -e], [e, c]]))
        inv.append(np.stack(per))
    return (
        xt,
        np.stack(fwd).astype(ml_dtypes.bfloat16),
        np.stack(inv).astype(ml_dtypes.bfloat16),
    )


def cos_poly(z, terms):
    acc = jnp.full_like(z, (-1.0) ** terms / math.factorial(2 * terms))
    for k in range(terms - 1, -1, -1):
        acc = acc * z + (-1.0) ** k / math.factorial(2 * k)
    return acc


def sinc_poly(z, terms):
    acc = jnp.full_like(z, (-1.0) ** terms / math.factorial(2 * terms + 1))
    for k in range(terms - 1, -1, -1):
        acc = acc * z + (-1.0) ** k / math.factorial(2 * k + 1)
    return acc


def call(kernel, grid, in_specs, out_specs, out_shape, scratch=(), flops=0):
    return pl.pallas_call(
        kernel,
        out_shape=out_shape,
        grid_spec=pltpu.PrefetchScalarGridSpec(
            num_scalar_prefetch=2,
            grid=grid,
            in_specs=in_specs,
            out_specs=out_specs,
            scratch_shapes=list(scratch),
        ),
        compiler_params=pltpu.CompilerParams(vmem_limit_bytes=VMEM_LIMIT),
        cost_estimate=pl.CostEstimate(
            flops=flops, bytes_accessed=4 * 1024 * 1024, transcendentals=0
        ),
    )


def start_kernel(ints, reals, packet_ref, out_ref, acc):
    core = ints[0]
    slab = 2 * pl.program_id(0) + core
    traces = packet_ref.shape[-1]
    chunk = 512
    acc[...] = jnp.zeros_like(acc)

    def add(i, carry):
        at = pl.ds(pl.multiple_of(i * chunk, chunk), chunk)
        cells = packet_ref[0, 2:3, at].astype(jnp.int32)
        line = cells // NX
        col = cells - line * NX
        ylines = lax.broadcasted_iota(jnp.int32, (SLAB, chunk), 0)
        hit = ylines == line
        vals = packet_ref[0, 0:2, at]
        left = jnp.concatenate(
            [jnp.where(hit, vals[c : c + 1], 0.0).astype(bf16) for c in range(2)], axis=0
        )
        for j in range(NX // TILE):
            xcols = lax.broadcasted_iota(jnp.int32, (TILE, chunk), 0) + j * TILE
            right = jnp.where(xcols == col, 1.0, 0.0).astype(bf16)
            acc[:, j * TILE : (j + 1) * TILE] += lax.dot_general(
                left, right, (((1,), (1,)), ((), ())), preferred_element_type=f32
            )
        return carry

    lax.fori_loop(0, traces // chunk, add, 0)
    out_ref[1] = acc[...].astype(bf16).reshape(2, SLAB, NX)

    strip = 32

    def source(i, carry):
        at = pl.ds(pl.multiple_of(i * strip, strip), strip)
        line = lax.broadcasted_iota(jnp.int32, (strip, NX), 0) + (
            slab * SLAB + i * strip - ints[2]
        )
        col = lax.broadcasted_iota(jnp.int32, (strip, NX), 1) - ints[3]
        dy = line.astype(f32) * grid_step
        dx = col.astype(f32) * grid_step
        radius = jnp.sqrt(dy * dy + dx * dx + datum_depth**2)
        amplitude = datum_depth / radius
        phase = reals[0] * (radius * water_slowness)
        turns = jnp.floor(phase * (0.5 / math.pi) + 0.5)
        rest = phase - turns * 6.28125
        rest = rest - turns * (2.0 * math.pi - 6.28125)
        z = rest * rest
        cosine = amplitude * cos_poly(z, 9)
        sine = amplitude * (rest * sinc_poly(z, 9))
        out_ref[0, 0, at, :] = (reals[1] * cosine - reals[2] * sine).astype(bf16)
        out_ref[0, 1, at, :] = (reals[1] * sine + reals[2] * cosine).astype(bf16)
        return carry

    lax.fori_loop(0, SLAB // strip, source, 0)


def start_fields(ints, reals, packets):
    traces = packets.shape[-1]
    return call(
        start_kernel,
        (2,),
        [pl.BlockSpec((1, 4, traces), lambda i, a, b: (i + a[1] - 2 * i * a[1], 0, 0))],
        pl.BlockSpec((2, 2, SLAB, NX), lambda i, a, b: (0, 0, i, 0)),
        jax.ShapeDtypeStruct((2, 2, 2 * SLAB, NX), bf16),
        [pltpu.VMEM((2 * SLAB, NX), f32)],
        flops=8_000_000_000,
    )(ints, reals, packets)


def forward_x_kernel(ints, reals, wave_ref, table_ref, out_ref):
    rows = wave_ref.shape[2]
    left = wave_ref[...].reshape(4 * rows, NX)
    cos_part = jnp.dot(left, table_ref[0], preferred_element_type=f32)
    sin_part = jnp.dot(left, table_ref[1], preferred_element_type=f32)
    cos_part = cos_part.reshape(2, 2, rows, -1)
    sin_part = sin_part.reshape(2, 2, rows, -1)
    out_ref[:, 0] = (cos_part[:, 0] + sin_part[:, 1]).astype(bf16)
    out_ref[:, 1] = (cos_part[:, 1] - sin_part[:, 0]).astype(bf16)


def forward_x(ints, reals, wave, table, other):
    def half(a):
        return (1 - a[0]) if other else a[0]

    rows = wave.shape[2]
    tiles = HALF // TILE
    return call(
        forward_x_kernel,
        (tiles,),
        [
            pl.BlockSpec((2, 2, rows, NX), lambda i, a, b: (0, 0, 0, 0)),
            pl.BlockSpec((2, NX, TILE), lambda i, a, b: (0, 0, half(a) * tiles + i)),
        ],
        pl.BlockSpec((2, 2, rows, TILE), lambda i, a, b: (0, 0, 0, i)),
        jax.ShapeDtypeStruct((2, 2, rows, HALF), bf16),
        flops=4_000_000_000,
    )(ints, reals, wave, table)


def middle_kernel(
    step, ints, reals, mine_ref, got_ref, fm_ref, fg_ref, im_ref, ig_ref, keep_ref, send_ref
):
    width = mine_ref.shape[-1]
    omega, slow, aniso = reals[0], reals[3 + step], reals[3 + STEPS + step]
    q = lax.broadcasted_iota(jnp.int32, (NY, width), 0)
    k = lax.broadcasted_iota(jnp.int32, (NY, width), 1)
    k = k + ints[0] * HALF + pl.program_id(0) * width
    q = jnp.where(q < NY // 2, q, q - NY).astype(f32) * (2.0 * math.pi / (NY * grid_step))
    k = jnp.where(k < NX // 2, k, k - NX).astype(f32) * (2.0 * math.pi / (NX * grid_step))
    base = omega * slow
    vertical = base * base - (1.0 + 2.0 * aniso) * (q * q + k * k)
    going = jnp.maximum(vertical, 0.0)
    z = going * (depth_step * depth_step)
    damping = jnp.exp(jnp.sqrt(jnp.maximum(-vertical, 0.0)) * (-depth_step))
    cosine = damping * cos_poly(z, 8)
    sine = damping * (jnp.sqrt(going) * depth_step * sinc_poly(z, 8))
    slabs = im_ref.shape[0]
    for g in range(2):
        spec = jnp.dot(
            fm_ref[0], mine_ref[g].reshape(4 * SLAB, width), preferred_element_type=f32
        ) + jnp.dot(fg_ref[0], got_ref[g].reshape(4 * SLAB, width), preferred_element_type=f32)
        re, im = spec[:NY], spec[NY:]
        sgn = sine if g == 0 else -sine
        shifted = jnp.concatenate(
            [(re * cosine - im * sgn).astype(bf16), (im * cosine + re * sgn).astype(bf16)], axis=0
        )
        for hi in range(slabs):
            at = slice(hi * SLAB, (hi + 1) * SLAB)
            for table, out in ((ig_ref, send_ref), (im_ref, keep_ref)):
                back = jnp.dot(table[hi, 0], shifted, preferred_element_type=f32).astype(bf16)
                out[g, 0, at] = back[:SLAB]
                out[g, 1, at] = back[SLAB:]


def middle(step, ints, reals, mine, got, fwd, inv):
    last = step == STEPS - 1
    slabs = 1 if last else 2
    rows = slabs * SLAB

    def low(a):
        return a[1] if last else 0

    width = TILE
    return call(
        functools.partial(middle_kernel, step),
        (HALF // width,),
        [
            pl.BlockSpec((2, 2, 2 * SLAB, width), lambda i, a, b: (0, 0, 0, i)),
            pl.BlockSpec((2, 2, 2 * SLAB, width), lambda i, a, b: (0, 0, 0, i)),
            pl.BlockSpec((1, 2 * NY, NY), lambda i, a, b: (a[0], 0, 0)),
            pl.BlockSpec((1, 2 * NY, NY), lambda i, a, b: (1 - a[0], 0, 0)),
            pl.BlockSpec((slabs, 1, 2 * SLAB, 2 * NY), lambda i, a, b: (low(a), a[0], 0, 0)),
            pl.BlockSpec((slabs, 1, 2 * SLAB, 2 * NY), lambda i, a, b: (low(a), 1 - a[0], 0, 0)),
        ],
        [pl.BlockSpec((2, 2, rows, width), lambda i, a, b: (0, 0, 0, i))] * 2,
        [jax.ShapeDtypeStruct((2, 2, rows, HALF), bf16)] * 2,
        flops=4_000_000_000,
    )(ints, reals, mine, got, fwd, fwd, inv, inv)


def inverse_x_kernel(
    step, ints, reals, keep_ref, got_ref, tm_ref, tg_ref, *refs
):
    *model_refs, block_ref, wave_ref, image_ref = refs
    rows = keep_ref.shape[2]
    mine = keep_ref[...].reshape(4 * rows, HALF)
    got = got_ref[...].reshape(4 * rows, HALF)
    omega, slow_ref = reals[0], reals[3 + step]
    cos_part = jnp.dot(mine, tm_ref[0], preferred_element_type=f32) + jnp.dot(
        got, tg_ref[0], preferred_element_type=f32
    )
    sin_part = jnp.dot(mine, tm_ref[1], preferred_element_type=f32) + jnp.dot(
        got, tg_ref[1], preferred_element_type=f32
    )
    cos_part = cos_part.reshape(2, 2, rows, TILE)
    sin_part = sin_part.reshape(2, 2, rows, TILE)
    space_re = cos_part[:, 0] - sin_part[:, 1]
    space_im = cos_part[:, 1] + sin_part[:, 0]
    matrix = block_ref[step]
    width = matrix.shape[0]
    slabs = rows // SLAB
    for j in range(TILE // width):
        at = slice(j * width, (j + 1) * width)
        near = model_refs[0][j].astype(f32)
        if slabs == 1:
            slow, aniso = near[0], near[1]
        else:
            far = model_refs[1][j].astype(f32)
            first = jnp.where(ints[1] == 0, near, far)
            second = jnp.where(ints[1] == 0, far, near)
            slow = jnp.concatenate([first[0], second[0]], axis=0)
            aniso = jnp.concatenate([first[1], second[1]], axis=0)
        phase = omega * (slow - slow_ref) * depth_step
        z = phase * phase
        cosine = cos_poly(z, 7)
        sine = phase * sinc_poly(z, 7)
        coefficient = omega * (slow * aniso) * depth_step
        nexts = []
        for g in range(2):
            sgn = sine if g == 0 else -sine
            re, im = space_re[g, :, at], space_im[g, :, at]
            split_re = (re * cosine - im * sgn).astype(bf16)
            split_im = (im * cosine + re * sgn).astype(bf16)
            both = jnp.concatenate([split_re, split_im], axis=0)
            correction = jnp.dot(both, matrix, preferred_element_type=f32)
            scaled = coefficient if g == 0 else -coefficient
            next_re = (split_re.astype(f32) - scaled * correction[rows:]).astype(bf16)
            next_im = (split_im.astype(f32) + scaled * correction[:rows]).astype(bf16)
            wave_ref[g, 0, :, at] = next_re
            wave_ref[g, 1, :, at] = next_im
            nexts.append((next_re.astype(f32), next_im.astype(f32)))
        image = nexts[0][0] * nexts[1][0] + nexts[0][1] * nexts[1][1]
        image_ref[:, at] = image.astype(bf16)


def inverse_x(step, ints, reals, keep, got, table, model, block):
    rows = keep.shape[2]
    width = block.shape[-1]

    return call(
        functools.partial(inverse_x_kernel, step),
        (NX // TILE,),
        [
            pl.BlockSpec((2, 2, rows, HALF), lambda i, a, b: (0, 0, 0, 0)),
            pl.BlockSpec((2, 2, rows, HALF), lambda i, a, b: (0, 0, 0, 0)),
            pl.BlockSpec((2, HALF, TILE), lambda i, a, b: (0, a[0], i)),
            pl.BlockSpec((2, HALF, TILE), lambda i, a, b: (0, 1 - a[0], i)),
        ]
        + [pl.BlockSpec((TILE // width, 2, SLAB, width), lambda i, a, b: (i, 0, 0, 0))]
        * len(model)
        + [
            pl.BlockSpec((STEPS, width, width), lambda i, a, b: (0, 0, 0)),
        ],
        [
            pl.BlockSpec((2, 2, rows, TILE), lambda i, a, b: (0, 0, 0, i)),
            pl.BlockSpec((rows, TILE), lambda i, a, b: (0, i)),
        ],
        [
            jax.ShapeDtypeStruct((2, 2, rows, NX), bf16),
            jax.ShapeDtypeStruct((rows, NX), bf16),
        ],
        flops=5_000_000_000,
    )(ints, reals, keep, got, table, table, *model, block)


def body(
    nfreq,
    nlat,
    record,
    receiver_cell,
    source_cell,
    wavelet,
    frequency_index,
    slowness,
    anisotropy,
    reference_slowness,
    reference_anisotropy,
    correction_block,
):
    fi = lax.axis_index("freq")
    zi = lax.axis_index("lat")
    core = fi % 2
    zh = zi // 2
    pair = [(i, i ^ 1) for i in range(nfreq)]
    swap = [
        ((2 * j + h) * nlat + 2 * a + c, (2 * j + c) * nlat + 2 * a + h)
        for j in range(nfreq // 2)
        for h in range(2)
        for a in range(nlat // 2)
        for c in range(2)
    ]
    cross = [
        ((2 * j + h) * nlat + 2 * a + c, (2 * j + c) * nlat + 2 * (1 - a) + h)
        for j in range(nfreq // 2)
        for h in range(2)
        for a in range(nlat // 2)
        for c in range(2)
    ]
    xt, fwd, inv = (jnp.asarray(t) for t in tables())

    both = ("freq", "lat")
    moved = lax.all_to_all(record.astype(bf16), "freq", split_axis=0, concat_axis=3, tiled=True)
    traces = receiver_cell.shape[-1]
    scalars = jnp.concatenate([frequency_index.astype(f32), wavelet.reshape(-1)])
    packet = jnp.concatenate(
        [
            moved.reshape(2, traces).astype(f32),
            receiver_cell.astype(f32),
            jnp.pad(scalars, (0, traces - 3))[None],
        ]
    )
    near = lax.ppermute(packet, both, swap)
    far = lax.ppermute(packet, both, cross)
    packets = jnp.stack([near, far])
    head = near[3, :3]
    angular = head[0] * (2.0 * math.pi * freq_step)

    models = []
    for s in range(STEPS):
        model = jnp.stack([slowness[s], anisotropy[s]]).astype(bf16)
        model = lax.all_gather(model, "freq")
        if s == 0:
            model, packets = lax.optimization_barrier((model, packets))
        width = model.shape[-1]
        if width != SLAB:
            model = model.transpose(1, 2, 0, 3).reshape(2, SLAB, NX // SLAB, SLAB)
            model = model.transpose(2, 0, 1, 3)
        model_near = lax.ppermute(model, both, swap)
        model = [model_near] if s == STEPS - 1 else [model_near, lax.ppermute(model, both, cross)]
        models.append(model)

    source_line = source_cell[0] // NX
    ints = jnp.stack([core, zh, source_line, source_cell[0] - source_line * NX]).astype(jnp.int32)
    reals = jnp.concatenate(
        [angular[None], head[1:3], reference_slowness, reference_anisotropy]
    )
    wave = start_fields(ints, reals, packets)
    images = []
    for s in range(STEPS):
        send = forward_x(ints, reals, wave, xt, True)
        got = lax.ppermute(send, "freq", pair)
        mine = forward_x(ints, reals, wave, xt, False)
        keep, send = middle(s, ints, reals, mine, got, fwd, inv)
        got = lax.ppermute(send, "freq", pair)
        wave, image = inverse_x(s, ints, reals, keep, got, xt, models[s], correction_block)
        if s < STEPS - 1:
            image = lax.dynamic_slice_in_dim(image, zh * SLAB, SLAB, 0)
        images.append(image)
    images = lax.ppermute(jnp.stack(images), both, swap)
    images = lax.all_to_all(
        images.reshape(STEPS, SLAB, nfreq, NX // nfreq).transpose(2, 0, 1, 3), "freq", 0, 0, tiled=True
    )
    wave = lax.ppermute(wave, both, swap)
    return jnp.sum(images.astype(f32), axis=0), wave[:, None]


def solution(mesh):
    return jax.shard_map(
        functools.partial(body, mesh.shape["freq"], mesh.shape["lat"]),
        mesh=mesh,
        in_specs=(
            P(None, None, "lat", "freq"),
            P("lat", None),
            P(),
            P("freq", None),
            P("freq"),
            P(None, "lat", "freq"),
            P(None, "lat", "freq"),
            P(),
            P(),
            P(),
        ),
        out_specs=(P(None, "lat", "freq"), P(None, "freq", None, "lat", None)),
        check_vma=False,
    )
```
